32 devices in a mesh: groups: 2 (over x), space: 16 (over z, y, core).
Axes of the slice: x: 2, y: 2, z: 4, core: 2. Of those that a mesh axis runs over, the one named last changes fastest.
Arguments:
- mol_feats: bfloat16 [8192, 512], P(('groups', 'space')), parts along dimension 0, may hold values from -6 to 6
- w_src: bfloat16 [512, 512], replicated, may hold values from -0.25 to 0.25
- w_dst: bfloat16 [512, 512], replicated, may hold values from -0.25 to 0.25
- w_out: bfloat16 [512, 529], replicated, may hold values from -0.25 to 0.25
- grad_blocks: bfloat16 [16, 32, 128, 529], P('space', 'groups'), parts along dimension 1, may hold values from -6 to 6
- edge_src: int32 [65536], P(('groups', 'space')), parts along dimension 0, may hold values from 0 to 255
- edge_dst: int32 [65536], P(('groups', 'space')), parts along dimension 0, may hold values from 0 to 383
- edge_live: int32 [65536], P(('groups', 'space')), parts along dimension 0, may hold values from 0 to 1, as said below
Outputs:
- feature_grad: float32 [8192, 512], P(('groups', 'space')), parts along dimension 0
- src_weight_grad: float32 [1024, 512], P(('groups', 'space')), parts along dimension 0
- dst_weight_grad: float32 [1024, 512], P(('groups', 'space')), parts along dimension 0
- out_weight_grad: float32 [1024, 529], P(('groups', 'space')), parts along dimension 0
The draws below stay inside these ranges and needn't reach their ends.
There are 2 independent parts, one for each index of `groups`. The reference program is written for one: setup_inputs(seed, part) draws one part's arguments, and reference() takes and returns one part's arrays. A program takes and returns all parts, laid end to end along the dimension named above; an argument that names none is the same for every part. Nothing has to cross between parts.
Inputs may be any that keep to these rules, and one draw needn't show every extreme that they name: `edge_live`: on every slab the live slots of each owner come first among its 128 slots, and the slab's own blocks fill all 128 of theirs. Any other owner has at most 64 live slots for a slab, and on every slab some other owner has exactly 64. `edge_dst`: index into the slab's molecules extended by 64 molecules of the slab below (first) and 64 of the slab above (last), periodic.
All inputs are finite; a program needn't handle non-finite values.
Results may differ from the reference program's by a relative error of at most 0.0029.
Values may be sent and summed in bfloat16 or wider, within the bound.
A program may use at most 64 MiB of HBM per device.

```python
import jax
import jax.numpy as jnp
from jax import lax

WIDTH = 512
BLOCK = 23
MOL_DEV = 256
EDGE_DEV = 2048
REACH = 64
CAP = 128
MOLS = 4096
EDGES = 32768
N_SPACE = 16


def draw_edge_live(key, part):
    half = CAP // 2
    counts = jax.random.randint(jax.random.fold_in(key, 7), (N_SPACE, N_SPACE), 3 * CAP // 8, half + 1)
    rows = jnp.arange(N_SPACE)[:, None]
    cols = jnp.arange(N_SPACE)[None, :]
    counts = jnp.where(cols == (rows + 1) % N_SPACE, half, counts)
    counts = jnp.where(rows == cols, CAP, counts)
    slots = jnp.arange(CAP)[None, None, :]
    live = (slots < counts[:, :, None]).astype(jnp.int32)
    return live.reshape(N_SPACE * N_SPACE * CAP)


def set_ends(values, stream_key, low, top_value):
    extent = values.shape
    spot = [jax.random.randint(jax.random.fold_in(stream_key, axis), (), 0, extent[axis]) for axis in range(len(extent))]
    values = values.at[tuple(spot)].set(low)
    longest = extent.index(max(extent))
    spot[longest] = (spot[longest] + 1) % extent[longest]
    return values.at[tuple(spot)].set(top_value)


def raised(result, key, source, target, parts, factor):
    owner, partner = [(jnp.arange(result.shape[position]) // (result.shape[position] // parts)).reshape([-1 if axis == position else 1 for axis in range(result.ndim)]) for position in (source, target)]
    chosen = jax.random.permutation(key, parts)[partner]
    strong = (owner == chosen) | (owner == (partner + parts // 2) % parts)
    return jnp.where(strong, factor * result, result)


def block_scale(own_key, dims, shards, smallest, largest):
    level = 1.0
    for dim, blocks in shards:
        draws = jax.random.uniform(jax.random.fold_in(jax.random.fold_in(own_key, 6), dim), (blocks,), jnp.float32, smallest / len(shards), largest / len(shards))
        level = level * jnp.repeat(jnp.exp(draws), dims[dim] // blocks).reshape((-1,) + (1,) * (len(dims) - 1 - dim))
    return level


def centred(key, dims, scale, reach, split=(), held_as=jnp.bfloat16):
    factor_of = block_scale(key, dims, split, -0.22, 0.18) if split else 1.0
    result = jax.random.normal(key, dims, jnp.float32) * scale * factor_of
    return jnp.minimum(jnp.maximum(result, -reach), reach).astype(held_as)


def bell_draw_with(key, extent, scale, limit, shards, heavy, held_as=jnp.bfloat16):
    drawn = scale * jax.random.normal(key, extent, jnp.float32)
    if shards:
        drawn = drawn * block_scale(key, extent, shards, -0.22, 0.18)
    return jnp.clip(raised(drawn, jax.random.fold_in(key, 3), *heavy), -limit, limit).astype(held_as)


def setup_inputs(seed: int = 0, part: int = 0) -> dict:
    key_list = jax.random.split(jax.random.key(seed), 9)
    own_keys = jax.random.split(jax.random.fold_in(key_list[8], part), 9)
    return {
        "mol_feats": bell_draw_with(own_keys[0], (MOLS, WIDTH), 1.0, 6.0, ((0, 16),), (0, 1, 16, 2.0)),
        "w_src": centred(key_list[1], (WIDTH, WIDTH), WIDTH ** -0.5, 0.25),
        "w_dst": centred(key_list[2], (WIDTH, WIDTH), WIDTH ** -0.5, 0.25),
        "w_out": centred(key_list[3], (WIDTH, BLOCK * BLOCK), WIDTH ** -0.5, 0.25),
        "grad_blocks": centred(own_keys[4], (N_SPACE, N_SPACE, CAP, BLOCK * BLOCK), 1.0, 6.0, ((0, 16),)),
        "edge_src": set_ends(jax.random.randint(own_keys[5], (EDGES,), 0, MOL_DEV), jax.random.fold_in(own_keys[5], 1), 0, MOL_DEV - 1).astype(jnp.int32),
        "edge_dst": set_ends(jax.random.randint(own_keys[6], (EDGES,), 0, MOL_DEV + 2 * REACH), jax.random.fold_in(own_keys[6], 1), 0, (MOL_DEV + 2 * REACH) - 1).astype(jnp.int32),
        "edge_live": draw_edge_live(jax.random.fold_in(jax.random.fold_in(key_list[8], part), 71), part),
    }


def reference(mol_feats, w_src, w_dst, w_out, grad_blocks, edge_src, edge_dst, edge_live):
    highest = lax.Precision.HIGHEST
    proj_src = jnp.dot(mol_feats, w_src, preferred_element_type=jnp.float32)
    proj_dst = jnp.dot(mol_feats, w_dst, preferred_element_type=jnp.float32)
    width = mol_feats.shape[1]
    entries = w_out.shape[1]

    def step(carry, inputs):
        src_sum, dst_sum, out_sum = carry
        index, local_src, local_dst, live = inputs
        src_rows = (index * MOL_DEV + local_src).astype(jnp.int32)
        dst_rows = ((index * MOL_DEV + local_dst - REACH) % MOLS).astype(jnp.int32)
        blocks = lax.dynamic_index_in_dim(grad_blocks, index, 1, keepdims=False).reshape(EDGE_DEV, entries)
        blocks = jnp.where(live[:, None] > 0, blocks, jnp.zeros_like(blocks))
        pre = proj_src[src_rows] + proj_dst[dst_rows]
        sigma = jax.nn.sigmoid(pre)
        hidden = (pre * sigma).astype(jnp.bfloat16)
        grad_hidden = jnp.dot(blocks, w_out.T, preferred_element_type=jnp.float32)
        grad_pre = (grad_hidden * sigma * (1.0 + pre * (1.0 - sigma))).astype(jnp.bfloat16)
        grad_wide = lax.optimization_barrier(grad_pre).astype(jnp.float32)
        src_sum = src_sum + jax.ops.segment_sum(grad_wide, src_rows, num_segments=MOLS)
        dst_sum = dst_sum + jax.ops.segment_sum(grad_wide, dst_rows, num_segments=MOLS)
        out_sum = out_sum + jnp.dot(hidden.T, blocks, preferred_element_type=jnp.float32)
        return (src_sum, dst_sum, out_sum), None

    start = (jnp.zeros((MOLS, width), jnp.float32), jnp.zeros((MOLS, width), jnp.float32), jnp.zeros((width, entries), jnp.float32))
    inputs = (jnp.arange(N_SPACE, dtype=jnp.int32), edge_src.reshape(N_SPACE, EDGE_DEV), edge_dst.reshape(N_SPACE, EDGE_DEV), edge_live.reshape(N_SPACE, EDGE_DEV))
    (src_sum, dst_sum, out_sum), unused = lax.scan(step, start, inputs)
    factor = float(EDGES) ** -0.5
    feats_wide = mol_feats.astype(jnp.float32)
    feature_grad = jnp.dot(src_sum, w_src.astype(jnp.float32).T, precision=highest) + jnp.dot(dst_sum, w_dst.astype(jnp.float32).T, precision=highest)
    src_weight_grad = factor * jnp.dot(feats_wide.T, src_sum, precision=highest)
    dst_weight_grad = factor * jnp.dot(feats_wide.T, dst_sum, precision=highest)
    out_weight_grad = factor * out_sum
    return (feature_grad, src_weight_grad, dst_weight_grad, out_weight_grad)
```

```python
import functools

import jax
import jax.numpy as jnp
from jax import lax
from jax.experimental import pallas as pl
from jax.experimental.pallas import tpu as pltpu
from jax.sharding import PartitionSpec as P

MESH = pl.DeviceIdType.MESH
F32 = jnp.float32
BF16 = jnp.bfloat16
NT = (((1,), (1,)), ((), ()))


def mm(a, b):
    return jnp.dot(a, b, preferred_element_type=F32)


def mm_nt(a, b):
    return lax.dot_general(a, b, NT, preferred_element_type=F32)


def split(x):
    high = x.astype(BF16)
    return high, (x - high.astype(F32)).astype(BF16)


def kernel(
    dims, feats, w_src, w_dst, w_out, idx, idx_own, blocks, fgrad, src_out, dst_out, out_out,
    halo, ext, own, recv, pt_hi, pt_lo, ft, oh, hid, fac, oh_own, hid_own, fac_own, sums, out_sum, back,
    block_send, block_recv, halo_send, halo_recv, back_send, back_recv, own_sem, *rs,
):
    n, half, mols, reach, factor, fused = dims
    quarter = n // 4
    chunk = quarter * half
    me = lax.axis_index("space")
    above = lax.rem(me + 1, n)
    below = lax.rem(me + n - 1, n)

    barrier = pltpu.get_barrier_semaphore()

    @pl.loop(1, n)
    def _(k):
        pl.semaphore_signal(barrier, inc=1, device_id={"space": lax.rem(me + k, n)}, device_id_type=MESH)

    local = pltpu.make_async_copy(blocks.at[0, me], own, own_sem)
    local.start()
    pl.semaphore_wait(barrier, n - 1)

    def remote(src, dst, send, arrive, device):
        return pltpu.make_async_remote_copy(
            src_ref=src, dst_ref=dst, send_sem=send, recv_sem=arrive,
            device_id={"space": device}, device_id_type=MESH,
        )

    def block_copy(source_slot, target):
        return remote(
            blocks.at[0, target, pl.ds(0, half)], recv.at[source_slot],
            block_send.at[target], block_recv.at[source_slot], target,
        )

    up = remote(feats.at[pl.ds(mols - reach, reach)], halo.at[0], halo_send.at[0], halo_recv.at[0], above)
    down = remote(feats.at[pl.ds(0, reach)], halo.at[1], halo_send.at[1], halo_recv.at[1], below)
    up.start()
    down.start()

    @pl.loop(1, n)
    def _(k):
        block_copy(me, lax.rem(me + k, n)).start()

    recv[me] = jnp.zeros(recv.shape[1:], BF16)
    ext[0:mols] = feats[...]
    pt = mm(feats[...], w_src[...]).T
    high, low = split(pt)
    pt_hi[:, 0:mols] = high
    pt_lo[:, 0:mols] = low
    up.wait()
    down.wait()
    ext[mols : mols + reach] = halo[0]
    ext[mols + reach : mols + 2 * reach] = halo[1]
    pt = mm(ext[...], w_dst[...]).T
    high, low = split(pt)
    pt_hi[:, mols:] = high
    pt_lo[:, mols:] = low
    ft[...] = ext[...].astype(F32).T.astype(BF16)

    def one_hot(ids, count):
        return (lax.broadcasted_iota(jnp.int32, (count, ids.shape[1]), 0) == ids).astype(F32).astype(BF16)

    def ahead(ids, oh_ref, hid_ref, fac_ref):
        oh_ref[0:mols] = one_hot(ids[0:1], mols)
        oh_ref[mols:] = one_hot(ids[1:2], mols + 2 * reach)
        pre = mm(pt_hi[...], oh_ref[...]) + mm(pt_lo[...], oh_ref[...])
        sigma = jax.nn.sigmoid(pre)
        hid_ref[...] = (pre * sigma).astype(BF16)
        fac_ref[...] = sigma * (1.0 + pre * (1.0 - sigma))

    def terms(g, oh_ref, hid_ref, fac_ref):
        dpre = (mm_nt(w_out[...], g) * fac_ref[...]).astype(BF16)
        return mm_nt(oh_ref[...], dpre), mm(hid_ref[...], g)

    ahead(idx_own[...], oh_own, hid_own, fac_own)
    local.wait()
    s, o = terms(own[...], oh_own, hid_own, fac_own)
    sums[...] = s
    out_sum[...] = o

    @pl.loop(0, 4)
    def _(c):
        ahead(idx[c], oh.at[c], hid.at[c], fac.at[c])

    @pl.loop(0, 4)
    def _(k):
        c = lax.rem(me // quarter + k, 4)

        @pl.loop(0, quarter)
        def _(j):
            owner = c * quarter + j

            @pl.when(owner != me)
            def _():
                block_copy(owner, lax.rem(owner + 0, n)).wait_recv()

        g = recv[pl.ds(c * quarter, quarter)].reshape(chunk, recv.shape[2])
        s, o = terms(g, oh.at[c], hid.at[c], fac.at[c])
        sums[...] += s
        out_sum[...] += o

    give_down = remote(sums.at[pl.ds(2 * mols, reach)], back.at[1], back_send.at[0], back_recv.at[1], below)
    give_up = remote(sums.at[pl.ds(2 * mols + reach, reach)], back.at[0], back_send.at[1], back_recv.at[0], above)

    def source_grad():
        high, low = split(sums[0:mols])
        return (mm(ft[:, 0:mols], high) + mm(ft[:, 0:mols], low)) * factor

    def target_grad():
        high, low = split(sums[mols:])
        return (mm(ft[...], high) + mm(ft[...], low)) * factor

    def feature_part():
        high, low = split(sums[0:mols])
        fgrad[...] = mm_nt(high, w_src[...]) + mm_nt(low, w_src[...])

    def feature_rest():
        give_down.wait()
        give_up.wait()
        total = jnp.concatenate(
            [
                sums[mols : mols + reach] + back[0],
                sums[mols + reach : 2 * mols - reach],
                sums[2 * mols - reach : 2 * mols] + back[1],
            ],
            axis=0,
        )
        high, low = split(total)
        fgrad[...] += mm_nt(high, w_dst[...]) + mm_nt(low, w_dst[...])

    if fused:
        chains = [rs[8 * a : 8 * a + 8] for a in range(3)]
        send_a, recv_a, send_b, recv_b, send_c, recv_c = rs[24:]
        core = lax.rem(me, 2)
        row = lax.rem(me // 2, 2)
        column = me // 4
        rows = out_out.shape[0]

        def stage_a(a, value):
            full, s1, r1 = chains[a][:3]
            value = value.reshape(quarter, 2, 2, rows, value.shape[1])
            for y in range(2):
                for p in range(2):
                    full[p, y] = value[:, y, p]
            s1[...] = full[1 - core].astype(BF16)
            copy_a(a).start()

        def copy_a(a):
            return remote(chains[a][1], chains[a][2], send_a.at[a], recv_a.at[a], me + 1 - 2 * core)

        def copy_b(a):
            return remote(chains[a][4], chains[a][5], send_b.at[a], recv_b.at[a], me + 2 - 4 * row)

        def stage_b(a):
            full, s1, r1, keep, s2 = chains[a][:5]
            copy_a(a).wait()
            s2[...] = (full[core, 1 - row] + r1[1 - row].astype(F32)).astype(BF16)
            copy_b(a).start()
            keep[...] = full[core, row] + r1[row].astype(F32)

        def copy_c(a, slot, target):
            return remote(
                chains[a][6].at[target], chains[a][7].at[slot], send_c.at[a, target], recv_c.at[a, slot],
                target * 4 + lax.rem(me, 4),
            )

        def stage_c(a):
            keep, s2, r2, s3, r3 = chains[a][3:]
            copy_b(a).wait()
            total = keep[...] + r2[...].astype(F32)
            keep[...] = total
            s3[...] = total.astype(BF16)

            @pl.loop(1, quarter)
            def _(k):
                copy_c(a, column, lax.rem(column + k, quarter)).start()

        def stage_d(a, result):
            keep, s2, r2, s3, r3 = chains[a][3:]
            r3[column] = jnp.zeros(r3.shape[1:], BF16)

            @pl.loop(1, quarter)
            def _(k):
                other = lax.rem(column + k, quarter)
                copy_c(a, other, other).wait()

            total = keep[column]
            for z in range(quarter):
                total = total + r3[z].astype(F32)
            result[...] = total

        stage_a(0, out_sum[...] * factor)
        give_down.start()
        give_up.start()
        stage_a(1, source_grad())
        stage_b(0)
        stage_a(2, target_grad())
        stage_b(1)
        stage_c(0)
        stage_b(2)
        feature_part()
        stage_c(1)
        feature_rest()
        stage_c(2)
        stage_d(0, out_out)
        stage_d(1, src_out)
        stage_d(2, dst_out)
    else:
        give_down.start()
        give_up.start()
        out_out[...] = out_sum[...] * factor
        src_out[...] = source_grad()
        dst_out[...] = target_grad()
        feature_part()
        feature_rest()

    @pl.loop(1, n)
    def _(k):
        block_copy(me, lax.rem(me + k, n)).wait_send()


def on_device(mol_feats, w_src, w_dst, w_out, grad_blocks, edge_src, edge_dst, edge_live):
    mols, width = mol_feats.shape
    entries = w_out.shape[1]
    reach = mols // 4
    n = grad_blocks.shape[1]
    cap = grad_blocks.shape[2]
    half = cap // 2
    quarter = n // 4
    chunk = quarter * half
    rows = width // n
    fused = rows % 16 == 0
    factor = float(edge_src.shape[0] * n) ** (-0.5)
    me = lax.axis_index("space")

    below = edge_dst < reach
    inside = edge_dst < reach + mols
    target = jnp.where(below, edge_dst + mols, jnp.where(inside, edge_dst - reach, edge_dst))
    ids = jnp.stack([edge_src, target]).reshape(2, n, cap)
    ids = jnp.where(edge_live.reshape(1, n, cap) > 0, ids, -1)
    idx_own = lax.dynamic_index_in_dim(ids, me, 1, keepdims=False)
    own_row = lax.broadcasted_iota(jnp.int32, (2, n, half), 1) == me
    idx = jnp.where(own_row, -1, ids[:, :, :half]).reshape(2, 4, chunk).transpose(1, 0, 2)

    span = mols + 2 * reach
    count = mols + span
    vm = pltpu.VMEM
    dma = pltpu.SemaphoreType.DMA
    scratch = [
        vm((2, reach, width), BF16),
        vm((span, width), BF16),
        vm((cap, entries), BF16),
        vm((n, half, entries), BF16),
        vm((width, count), BF16),
        vm((width, count), BF16),
        vm((width, span), BF16),
        vm((4, count, chunk), BF16),
        vm((4, width, chunk), BF16),
        vm((4, width, chunk), F32),
        vm((count, cap), BF16),
        vm((width, cap), BF16),
        vm((width, cap), F32),
        vm((count, width), F32),
        vm((width, entries), F32),
        vm((2, reach, width), F32),
        dma((n,)), dma((n,)), dma((2,)), dma((2,)), dma((2,)), dma((2,)), dma(()),
    ]
    if fused:
        for columns in (entries, width, width):
            piece = (quarter, rows, columns)
            scratch += [
                vm((2, 2) + piece, F32),
                vm((2,) + piece, BF16),
                vm((2,) + piece, BF16),
                vm(piece, F32),
                vm(piece, BF16),
                vm(piece, BF16),
                vm(piece, BF16),
                vm(piece, BF16),
            ]
        scratch += [dma((3,)), dma((3,)), dma((3,)), dma((3,)), dma((3, quarter)), dma((3, quarter))]
    out_rows = rows if fused else width
    whole = pl.BlockSpec(memory_space=pltpu.VMEM)
    fgrad, src_g, dst_g, out_g = pl.pallas_call(
        functools.partial(kernel, (n, half, mols, reach, factor, fused)),
        out_shape=(
            jax.ShapeDtypeStruct((mols, width), F32),
            jax.ShapeDtypeStruct((out_rows, width), F32),
            jax.ShapeDtypeStruct((out_rows, width), F32),
            jax.ShapeDtypeStruct((out_rows, entries), F32),
        ),
        in_specs=[whole] * 6 + [pl.BlockSpec(memory_space=pl.ANY)],
        out_specs=(whole,) * 4,
        scratch_shapes=scratch,
        compiler_params=pltpu.CompilerParams(
            collective_id=0, has_side_effects=True, vmem_limit_bytes=48 * 1024 * 1024
        ),
    )(mol_feats, w_src, w_dst, w_out, idx, idx_own, grad_blocks)
    if not fused:
        src_g, dst_g, out_g = [
            lax.psum_scatter(part, "space", scatter_dimension=0, tiled=True) for part in (src_g, dst_g, out_g)
        ]
    return fgrad, src_g, dst_g, out_g


def solution(mesh):
    placed = (
        P(("groups", "space"), None),
        P(),
        P(),
        P(),
        P("space", "groups", None, None),
        P(("groups", "space")),
        P(("groups", "space")),
        P(("groups", "space")),
    )
    return jax.shard_map(
        on_device,
        mesh=mesh,
        in_specs=placed,
        out_specs=(P(("groups", "space"), None),) * 4,
        check_vma=False,
    )
```

```python
import functools

import jax
import jax.numpy as jnp
from jax import lax
from jax.experimental import pallas as pl
from jax.experimental.pallas import tpu as pltpu
from jax.sharding import PartitionSpec as P

MESH = pl.DeviceIdType.MESH
F32 = jnp.float32
BF16 = jnp.bfloat16
NT = (((1,), (1,)), ((), ()))


def mm(a, b):
    return jnp.dot(a, b, preferred_element_type=F32)


def mm_nt(a, b):
    return lax.dot_general(a, b, NT, preferred_element_type=F32)


def split(x):
    high = x.astype(BF16)
    return high, (x - high.astype(F32)).astype(BF16)


def kernel(
    dims, feats_far, w_src_far, w_dst_far, w_out_t, idx, idx_own, own, blocks, tails, fgrad, src_out, dst_out, out_out,
    feats, w_src, w_dst, w_main, w_tail, halo, ext, recv, recv_tail, pt_hi, pt_lo, ft, oh, hid, fac, oh_own, hid_own,
    fac_own, sums, out_sum, back, block_send, block_recv, tail_send, tail_recv, halo_send, halo_recv, back_send,
    back_recv, load_sem, *rs,
):
    n, half, mols, reach, factor, fused, pack, base = dims
    quarter = n // 4
    chunk = quarter * half
    me = lax.axis_index("space")
    above = lax.rem(me + 1, n)
    below = lax.rem(me + n - 1, n)

    barrier = pltpu.get_barrier_semaphore()

    @pl.loop(1, n)
    def _(k):
        pl.semaphore_signal(barrier, inc=1, device_id={"space": lax.rem(me + k, n)}, device_id_type=MESH)

    loads = [
        pltpu.make_async_copy(far, near, load_sem.at[i])
        for i, (far, near) in enumerate(((feats_far, feats), (w_src_far, w_src), (w_dst_far, w_dst)))
    ]
    for load in loads:
        load.start()
    pl.semaphore_wait(barrier, n - 1)

    def remote(src, dst, send, arrive, device):
        return pltpu.make_async_remote_copy(
            src_ref=src, dst_ref=dst, send_sem=send, recv_sem=arrive,
            device_id={"space": device}, device_id_type=MESH,
        )

    def block_copy(source_slot, target):
        return remote(
            blocks.at[target], recv.at[source_slot], block_send.at[target], block_recv.at[source_slot], target
        )

    def tail_copy(source_slot, target):
        return remote(
            tails.at[target], recv_tail.at[source_slot], tail_send.at[target], tail_recv.at[source_slot], target
        )

    up = remote(feats_far.at[pl.ds(mols - reach, reach)], halo.at[0], halo_send.at[0], halo_recv.at[0], above)
    down = remote(feats_far.at[pl.ds(0, reach)], halo.at[1], halo_send.at[1], halo_recv.at[1], below)
    up.start()
    down.start()

    @pl.loop(1, n)
    def _(k):
        block_copy(me, lax.rem(me + k, n)).start()
        tail_copy(me, lax.rem(me + k, n)).start()

    recv[me] = jnp.zeros(recv.shape[1:], BF16)
    recv_tail[me] = jnp.zeros(recv_tail.shape[1:], BF16)
    width = w_main.shape[0]
    rest = w_out_t.shape[0] - width
    w_main[...] = w_out_t[0:width].astype(F32).T.astype(BF16)
    last = w_out_t[width:].astype(F32)
    last = jnp.concatenate([last, jnp.zeros((w_tail.shape[1] - rest, width), F32)], axis=0)
    w_tail[...] = last.T.astype(BF16)
    for load in loads:
        load.wait()
    ext[0:mols] = feats[...]
    pt = mm(feats[...], w_src[...]).T
    high, low = split(pt)
    pt_hi[:, 0:mols] = high
    pt_lo[:, 0:mols] = low
    up.wait()
    down.wait()
    ext[mols : mols + reach] = halo[0]
    ext[mols + reach : mols + 2 * reach] = halo[1]
    pt = mm(ext[...], w_dst[...]).T
    high, low = split(pt)
    pt_hi[:, mols:] = high
    pt_lo[:, mols:] = low
    ft[...] = ext[...].astype(F32).T.astype(BF16)

    def one_hot(ids, count):
        return (lax.broadcasted_iota(jnp.int32, (count, ids.shape[1]), 0) == ids).astype(F32).astype(BF16)

    def ahead(ids, oh_ref, hid_ref, fac_ref):
        oh_ref[0:mols] = one_hot(lax.shift_right_arithmetic(ids, base), mols)
        oh_ref[mols:] = one_hot(ids & ((1 << base) - 1), mols + 2 * reach)
        pre = mm(pt_hi[...], oh_ref[...]) + mm(pt_lo[...], oh_ref[...])
        sigma = jax.nn.sigmoid(pre)
        hid_ref[...] = (pre * sigma).astype(BF16)
        fac_ref[...] = sigma * (1.0 + pre * (1.0 - sigma))

    def terms(g, tail, oh_ref, hid_ref, fac_ref):
        dhidden = mm_nt(w_main[...], g) + mm_nt(w_tail[...], tail)
        dpre = (dhidden * fac_ref[...]).astype(BF16)
        return mm_nt(oh_ref[...], dpre), mm(hid_ref[...], g), mm(hid_ref[...], tail)[:, 0:rest]

    ahead(idx_own[...], oh_own, hid_own, fac_own)
    s, o, t = terms(own[:, 0:width], own[:, width:], oh_own, hid_own, fac_own)
    sums[...] = s
    out_sum[:, 0:width] = o
    out_sum[:, width:] = t

    @pl.loop(0, 4)
    def _(c):
        ahead(idx[c], oh.at[c], hid.at[c], fac.at[c])

    @pl.loop(0, 4)
    def _(k):
        c = lax.rem(me // quarter + k, 4)

        @pl.loop(0, quarter)
        def _(j):
            owner = c * quarter + j

            @pl.when(owner != me)
            def _():
                block_copy(owner, owner).wait_recv()
                tail_copy(owner, owner).wait_recv()

        g = recv[pl.ds(c * quarter, quarter)].reshape(quarter, pack, half // pack, width)
        g = jnp.concatenate([g[:, p].reshape(chunk // pack, width) for p in range(pack)], axis=0)
        tail = recv_tail[pl.ds(c * quarter, quarter)].reshape(chunk // pack, recv_tail.shape[2]).astype(F32)
        span = w_tail.shape[1]
        tail = jnp.concatenate([tail[:, p * span : (p + 1) * span] for p in range(pack)], axis=0).astype(BF16)
        s, o, t = terms(g, tail, oh.at[c], hid.at[c], fac.at[c])
        sums[...] += s
        out_sum[:, 0:width] += o
        out_sum[:, width:] += t

    give_down = remote(sums.at[pl.ds(2 * mols, reach)], back.at[1], back_send.at[0], back_recv.at[1], below)
    give_up = remote(sums.at[pl.ds(2 * mols + reach, reach)], back.at[0], back_send.at[1], back_recv.at[0], above)

    def source_grad():
        high, low = split(sums[0:mols])
        return (mm(ft[:, 0:mols], high) + mm(ft[:, 0:mols], low)) * factor

    def target_grad():
        high, low = split(sums[mols:])
        return (mm(ft[...], high) + mm(ft[...], low)) * factor

    def feature_part():
        high, low = split(sums[0:mols])
        fgrad[...] = mm_nt(high, w_src[...]) + mm_nt(low, w_src[...])

    def feature_rest():
        give_down.wait()
        give_up.wait()
        total = jnp.concatenate(
            [
                sums[mols : mols + reach] + back[0],
                sums[mols + reach : 2 * mols - reach],
                sums[2 * mols - reach : 2 * mols] + back[1],
            ],
            axis=0,
        )
        high, low = split(total)
        fgrad[...] += mm_nt(high, w_dst[...]) + mm_nt(low, w_dst[...])

    if fused:
        chains = [rs[8 * a : 8 * a + 8] for a in range(3)]
        send_a, recv_a, send_b, recv_b, send_c, recv_c = rs[24:]
        core = lax.rem(me, 2)
        row = lax.rem(me // 2, 2)
        column = me // 4
        rows = out_out.shape[0]

        def stage_a(a, value):
            full, s1, r1 = chains[a][:3]
            value = value.reshape(quarter, 2, 2, rows, value.shape[1])
            for y in range(2):
                for p in range(2):
                    full[p, y] = value[:, y, p]
            s1[...] = full[1 - core].astype(BF16)
            copy_a(a).start()

        def copy_a(a):
            return remote(chains[a][1], chains[a][2], send_a.at[a], recv_a.at[a], me + 1 - 2 * core)

        def copy_b(a):
            return remote(chains[a][4], chains[a][5], send_b.at[a], recv_b.at[a], me + 2 - 4 * row)

        def stage_b(a):
            full, s1, r1, keep, s2 = chains[a][:5]
            copy_a(a).wait()
            s2[...] = (full[core, 1 - row] + r1[1 - row].astype(F32)).astype(BF16)
            copy_b(a).start()
            keep[...] = full[core, row] + r1[row].astype(F32)

        def copy_c(a, slot, target):
            return remote(
                chains[a][6].at[target], chains[a][7].at[slot], send_c.at[a, target], recv_c.at[a, slot],
                target * 4 + lax.rem(me, 4),
            )

        def stage_c(a):
            keep, s2, r2, s3, r3 = chains[a][3:]
            copy_b(a).wait()
            total = keep[...] + r2[...].astype(F32)
            keep[...] = total
            s3[...] = total.astype(BF16)

            @pl.loop(1, quarter)
            def _(k):
                copy_c(a, column, lax.rem(column + k, quarter)).start()

        def stage_d(a, result):
            keep, s2, r2, s3, r3 = chains[a][3:]
            r3[column] = jnp.zeros(r3.shape[1:], BF16)

            @pl.loop(1, quarter)
            def _(k):
                other = lax.rem(column + k, quarter)
                copy_c(a, other, other).wait()

            total = keep[column]
            for z in range(quarter):
                total = total + r3[z].astype(F32)
            result[...] = total

        stage_a(0, out_sum[...] * factor)
        give_down.start()
        give_up.start()
        stage_a(1, source_grad())
        stage_b(0)
        stage_a(2, target_grad())
        stage_b(1)
        stage_c(0)
        stage_b(2)
        feature_part()
        stage_c(1)
        feature_rest()
        stage_c(2)
        stage_d(0, out_out)
        stage_d(1, src_out)
        stage_d(2, dst_out)
    else:
        give_down.start()
        give_up.start()
        out_out[...] = out_sum[...] * factor
        src_out[...] = source_grad()
        dst_out[...] = target_grad()
        feature_part()
        feature_rest()

    @pl.loop(1, n)
    def _(k):
        block_copy(me, lax.rem(me + k, n)).wait_send()
        tail_copy(me, lax.rem(me + k, n)).wait_send()


def on_device(mol_feats, w_src, w_dst, w_out, grad_blocks, edge_src, edge_dst, edge_live):
    mols, width = mol_feats.shape
    entries = w_out.shape[1]
    reach = mols // 4
    n = grad_blocks.shape[1]
    cap = grad_blocks.shape[2]
    half = cap // 2
    quarter = n // 4
    chunk = quarter * half
    rows = width // n
    fused = rows % 16 == 0
    factor = float(edge_src.shape[0] * n) ** (-0.5)
    me = lax.axis_index("space")

    below = edge_dst < reach
    inside = edge_dst < reach + mols
    target = jnp.where(below, edge_dst + mols, jnp.where(inside, edge_dst - reach, edge_dst))
    base = (mols + 2 * reach).bit_length()
    ids = jnp.where(edge_live > 0, (edge_src << base) + target, -1).reshape(n, cap)
    pack = 4 if half % 64 == 0 else 1
    tail_span = 128 // pack
    idx_own = lax.dynamic_slice_in_dim(ids, me, 1, axis=0)
    own_row = lax.broadcasted_iota(jnp.int32, (n, half), 0) == me
    idx = jnp.where(own_row, -1, ids[:, :half]).reshape(4, quarter, pack, half // pack)
    idx = idx.transpose(0, 2, 1, 3).reshape(4, 1, chunk)
    first = grad_blocks[0, :, :half]
    blocks = first[:, :, :width]
    rest = entries - width
    tails = jnp.pad(first[:, :, width:], ((0, 0), (0, 0), (0, tail_span - rest)))
    tails = tails.reshape(n, pack, half // pack, tail_span).transpose(0, 2, 1, 3).reshape(n, half // pack, 128)
    own = lax.dynamic_index_in_dim(grad_blocks[0], me, 0, keepdims=False)
    own = jnp.pad(own, ((0, 0), (0, tail_span - rest)))

    span = mols + 2 * reach
    count = mols + span
    vm = pltpu.VMEM
    dma = pltpu.SemaphoreType.DMA
    scratch = [
        vm((mols, width), BF16),
        vm((width, width), BF16),
        vm((width, width), BF16),
        vm((width, width), BF16),
        vm((width, tail_span), BF16),
        vm((2, reach, width), BF16),
        vm((span, width), BF16),
        vm((n, half, width), BF16),
        vm((n, half // pack, 128), BF16),
        vm((width, count), BF16),
        vm((width, count), BF16),
        vm((width, span), BF16),
        vm((4, count, chunk), BF16),
        vm((4, width, chunk), BF16),
        vm((4, width, chunk), F32),
        vm((count, cap), BF16),
        vm((width, cap), BF16),
        vm((width, cap), F32),
        vm((count, width), F32),
        vm((width, entries), F32),
        vm((2, reach, width), F32),
        dma((n,)), dma((n,)), dma((n,)), dma((n,)), dma((2,)), dma((2,)), dma((2,)), dma((2,)), dma((3,)),
    ]
    if fused:
        for columns in (entries, width, width):
            piece = (quarter, rows, columns)
            scratch += [
                vm((2, 2) + piece, F32),
                vm((2,) + piece, BF16),
                vm((2,) + piece, BF16),
                vm(piece, F32),
                vm(piece, BF16),
                vm(piece, BF16),
                vm(piece, BF16),
                vm(piece, BF16),
            ]
        scratch += [dma((3,)), dma((3,)), dma((3,)), dma((3,)), dma((3, quarter)), dma((3, quarter))]
    out_rows = rows if fused else width
    whole = pl.BlockSpec(memory_space=pltpu.VMEM)
    near = pl.BlockSpec(memory_space=pl.ANY)
    far = pl.BlockSpec(memory_space=pltpu.HBM)
    fgrad, src_g, dst_g, out_g = pl.pallas_call(
        functools.partial(kernel, (n, half, mols, reach, factor, fused, pack, base)),
        out_shape=(
            jax.ShapeDtypeStruct((mols, width), F32),
            jax.ShapeDtypeStruct((out_rows, width), F32),
            jax.ShapeDtypeStruct((out_rows, width), F32),
            jax.ShapeDtypeStruct((out_rows, entries), F32),
        ),
        in_specs=[far] * 3 + [whole] * 4 + [near] * 2,
        out_specs=(whole,) * 4,
        scratch_shapes=scratch,
        compiler_params=pltpu.CompilerParams(
            collective_id=0, has_side_effects=True, vmem_limit_bytes=48 * 1024 * 1024
        ),
    )(mol_feats, w_src, w_dst, w_out.T, idx, idx_own, own, blocks, tails)
    if not fused:
        src_g, dst_g, out_g = [
            lax.psum_scatter(part, "space", scatter_dimension=0, tiled=True) for part in (src_g, dst_g, out_g)
        ]
    return fgrad, src_g, dst_g, out_g


def solution(mesh):
    placed = (
        P(("groups", "space"), None),
        P(),
        P(),
        P(),
        P("space", "groups", None, None),
        P(("groups", "space")),
        P(("groups", "space")),
        P(("groups", "space")),
    )
    return jax.shard_map(
        on_device,
        mesh=mesh,
        in_specs=placed,
        out_specs=(P(("groups", "space"), None),) * 4,
        check_vma=False,
    )
```

```python
import functools

import jax
import jax.numpy as jnp
from jax import lax
from jax.experimental import pallas as pl
from jax.experimental.pallas import tpu as pltpu
from jax.sharding import PartitionSpec as P

MESH = pl.DeviceIdType.MESH
F32 = jnp.float32
BF16 = jnp.bfloat16
NT = (((1,), (1,)), ((), ()))


def mm(a, b):
    return jnp.dot(a, b, preferred_element_type=F32)


def mm_nt(a, b):
    return lax.dot_general(a, b, NT, preferred_element_type=F32)


def split(x):
    high = x.astype(BF16)
    return high, (x - high.astype(F32)).astype(BF16)


def kernel(
    dims, feats_far, w_src_far, w_dst_far, w_out_t, idx, idx_own, blocks, tails, fgrad, src_out, dst_out, out_out,
    own, feats, w_src, w_dst, w_main, w_tail, halo, ext, recv, recv_tail, pt_hi, pt_lo, ft, oh, hid, fac, oh_own, hid_own,
    fac_own, sums, out_sum, back, block_send, block_recv, tail_send, tail_recv, halo_send, halo_recv, back_send,
    back_recv, load_sem, *rs,
):
    n, half, mols, reach, factor, fused, pack, base = dims
    quarter = n // 4
    chunk = quarter * half
    width = w_main.shape[0]
    me = lax.axis_index("space")
    above = lax.rem(me + 1, n)
    below = lax.rem(me + n - 1, n)

    barrier = pltpu.get_barrier_semaphore()

    @pl.loop(1, n)
    def _(k):
        pl.semaphore_signal(barrier, inc=1, device_id={"space": lax.rem(me + k, n)}, device_id_type=MESH)

    pairs = ((feats_far, feats), (w_src_far, w_src), (w_dst_far, w_dst), (blocks.at[me], own))
    loads = [pltpu.make_async_copy(far, near, load_sem.at[i]) for i, (far, near) in enumerate(pairs)]
    for load in loads:
        load.start()
    pl.semaphore_wait(barrier, n - 1)

    def remote(src, dst, send, arrive, device):
        return pltpu.make_async_remote_copy(
            src_ref=src, dst_ref=dst, send_sem=send, recv_sem=arrive,
            device_id={"space": device}, device_id_type=MESH,
        )

    def block_copy(source_slot, target):
        return remote(
            blocks.at[target, pl.ds(0, half), pl.ds(0, width)], recv.at[source_slot],
            block_send.at[target], block_recv.at[source_slot], target,
        )

    def tail_copy(source_slot, target):
        return remote(
            tails.at[target], recv_tail.at[source_slot], tail_send.at[target], tail_recv.at[source_slot], target
        )

    up = remote(feats_far.at[pl.ds(mols - reach, reach)], halo.at[0], halo_send.at[0], halo_recv.at[0], above)
    down = remote(feats_far.at[pl.ds(0, reach)], halo.at[1], halo_send.at[1], halo_recv.at[1], below)
    up.start()
    down.start()

    @pl.loop(1, n)
    def _(k):
        target = lax.rem(me + 7 * k, n)
        block_copy(me, target).start()
        tail_copy(me, target).start()

    recv[me] = jnp.zeros(recv.shape[1:], BF16)
    recv_tail[me] = jnp.zeros(recv_tail.shape[1:], BF16)
    rest = w_out_t.shape[0] - width
    w_main[...] = w_out_t[0:width].astype(F32).T.astype(BF16)
    last = w_out_t[width:].astype(F32)
    last = jnp.concatenate([last, jnp.zeros((w_tail.shape[1] - rest, width), F32)], axis=0)
    w_tail[...] = last.T.astype(BF16)
    for load in loads:
        load.wait()
    ext[0:mols] = feats[...]
    pt = mm(feats[...], w_src[...]).T
    high, low = split(pt)
    pt_hi[:, 0:mols] = high
    pt_lo[:, 0:mols] = low
    up.wait()
    down.wait()
    ext[mols : mols + reach] = halo[0]
    ext[mols + reach : mols + 2 * reach] = halo[1]
    pt = mm(ext[...], w_dst[...]).T
    high, low = split(pt)
    pt_hi[:, mols:] = high
    pt_lo[:, mols:] = low
    ft[...] = ext[...].astype(F32).T.astype(BF16)

    def one_hot(ids, count):
        return (lax.broadcasted_iota(jnp.int32, (count, ids.shape[1]), 0) == ids).astype(F32).astype(BF16)

    def ahead(ids, oh_ref, hid_ref, fac_ref):
        oh_ref[0:mols] = one_hot(lax.shift_right_arithmetic(ids, base), mols)
        oh_ref[mols:] = one_hot(ids & ((1 << base) - 1), mols + 2 * reach)
        pre = mm(pt_hi[...], oh_ref[...]) + mm(pt_lo[...], oh_ref[...])
        sigma = jax.nn.sigmoid(pre)
        hid_ref[...] = (pre * sigma).astype(BF16)
        fac_ref[...] = sigma * (1.0 + pre * (1.0 - sigma))

    def terms(g, tail, oh_ref, hid_ref, fac_ref):
        dhidden = mm_nt(w_main[...], g) + mm_nt(w_tail[...], tail)
        dpre = (dhidden * fac_ref[...]).astype(BF16)
        return mm_nt(oh_ref[...], dpre), mm(hid_ref[...], g), mm(hid_ref[...], tail)[:, 0:rest]

    own_tail = jnp.concatenate(
        [own[:, width:].astype(F32), jnp.zeros((own.shape[0], w_tail.shape[1] - rest), F32)], axis=1
    ).astype(BF16)
    ahead(idx_own[...], oh_own, hid_own, fac_own)
    s, o, t = terms(own[:, 0:width], own_tail, oh_own, hid_own, fac_own)
    sums[...] = s
    out_sum[:, 0:width] = o
    out_sum[:, width:] = t

    @pl.loop(0, 4)
    def _(c):
        ahead(idx[c], oh.at[c], hid.at[c], fac.at[c])

    @pl.loop(0, 4)
    def _(k):
        c = lax.rem(me // quarter + k, 4)

        @pl.loop(0, quarter)
        def _(j):
            owner = c * quarter + j

            @pl.when(owner != me)
            def _():
                block_copy(owner, owner).wait_recv()
                tail_copy(owner, owner).wait_recv()

        g = recv[pl.ds(c * quarter, quarter)].reshape(quarter, pack, half // pack, width)
        g = jnp.concatenate([g[:, p].reshape(chunk // pack, width) for p in range(pack)], axis=0)
        tail = recv_tail[pl.ds(c * quarter, quarter)].reshape(chunk // pack, recv_tail.shape[2]).astype(F32)
        span = w_tail.shape[1]
        tail = jnp.concatenate([tail[:, p * span : (p + 1) * span] for p in range(pack)], axis=0).astype(BF16)
        s, o, t = terms(g, tail, oh.at[c], hid.at[c], fac.at[c])
        sums[...] += s
        out_sum[:, 0:width] += o
        out_sum[:, width:] += t

    give_down = remote(sums.at[pl.ds(2 * mols, reach)], back.at[1], back_send.at[0], back_recv.at[1], below)
    give_up = remote(sums.at[pl.ds(2 * mols + reach, reach)], back.at[0], back_send.at[1], back_recv.at[0], above)

    def source_grad():
        high, low = split(sums[0:mols])
        return (mm(ft[:, 0:mols], high) + mm(ft[:, 0:mols], low)) * factor

    def target_grad():
        high, low = split(sums[mols:])
        return (mm(ft[...], high) + mm(ft[...], low)) * factor

    def feature_part():
        high, low = split(sums[0:mols])
        fgrad[...] = mm_nt(high, w_src[...]) + mm_nt(low, w_src[...])

    def feature_rest():
        give_down.wait()
        give_up.wait()
        total = jnp.concatenate(
            [
                sums[mols : mols + reach] + back[0],
                sums[mols + reach : 2 * mols - reach],
                sums[2 * mols - reach : 2 * mols] + back[1],
            ],
            axis=0,
        )
        high, low = split(total)
        fgrad[...] += mm_nt(high, w_dst[...]) + mm_nt(low, w_dst[...])

    if fused:
        chains = [rs[8 * a : 8 * a + 8] for a in range(3)]
        send_a, recv_a, send_b, recv_b, send_c, recv_c = rs[24:]
        core = lax.rem(me, 2)
        row = lax.rem(me // 2, 2)
        column = me // 4
        rows = out_out.shape[0]

        def stage_a(a, value):
            full, s1, r1 = chains[a][:3]
            value = value.reshape(quarter, 2, 2, rows, value.shape[1])
            for y in range(2):
                for p in range(2):
                    full[p, y] = value[:, y, p]
            s1[...] = full[1 - core].astype(BF16)
            copy_a(a).start()

        def copy_a(a):
            return remote(chains[a][1], chains[a][2], send_a.at[a], recv_a.at[a], me + 1 - 2 * core)

        def copy_b(a):
            return remote(chains[a][4], chains[a][5], send_b.at[a], recv_b.at[a], me + 2 - 4 * row)

        def stage_b(a):
            full, s1, r1, keep, s2 = chains[a][:5]
            copy_a(a).wait()
            s2[...] = (full[core, 1 - row] + r1[1 - row].astype(F32)).astype(BF16)
            copy_b(a).start()
            keep[...] = full[core, row] + r1[row].astype(F32)

        def copy_c(a, slot, target):
            return remote(
                chains[a][6].at[target], chains[a][7].at[slot], send_c.at[a, target], recv_c.at[a, slot],
                target * 4 + lax.rem(me, 4),
            )

        def stage_c(a):
            keep, s2, r2, s3, r3 = chains[a][3:]
            copy_b(a).wait()
            total = keep[...] + r2[...].astype(F32)
            keep[...] = total
            s3[...] = total.astype(BF16)

            @pl.loop(1, quarter)
            def _(k):
                copy_c(a, column, lax.rem(column + k, quarter)).start()

        def stage_d(a, result):
            keep, s2, r2, s3, r3 = chains[a][3:]
            r3[column] = jnp.zeros(r3.shape[1:], BF16)

            @pl.loop(1, quarter)
            def _(k):
                other = lax.rem(column + k, quarter)
                copy_c(a, other, other).wait()

            total = keep[column]
            for z in range(quarter):
                total = total + r3[z].astype(F32)
            result[...] = total

        stage_a(0, out_sum[...] * factor)
        give_down.start()
        give_up.start()
        stage_a(1, source_grad())
        stage_b(0)
        stage_a(2, target_grad())
        stage_b(1)
        stage_c(0)
        stage_b(2)
        feature_part()
        stage_c(1)
        feature_rest()
        stage_c(2)
        stage_d(0, out_out)
        stage_d(1, src_out)
        stage_d(2, dst_out)
    else:
        give_down.start()
        give_up.start()
        out_out[...] = out_sum[...] * factor
        src_out[...] = source_grad()
        dst_out[...] = target_grad()
        feature_part()
        feature_rest()

    @pl.loop(1, n)
    def _(k):
        block_copy(me, lax.rem(me + k, n)).wait_send()
        tail_copy(me, lax.rem(me + k, n)).wait_send()


def write_out(*refs):
    copies = [pltpu.make_async_copy(refs[i], refs[4 + i], refs[8].at[i]) for i in range(4)]
    for copy in copies:
        copy.start()
    for copy in copies:
        copy.wait()


def on_device(mol_feats, w_src, w_dst, w_out, grad_blocks, edge_src, edge_dst, edge_live):
    mols, width = mol_feats.shape
    entries = w_out.shape[1]
    reach = mols // 4
    n = grad_blocks.shape[1]
    cap = grad_blocks.shape[2]
    half = cap // 2
    quarter = n // 4
    chunk = quarter * half
    rows = width // n
    fused = rows % 16 == 0
    factor = float(edge_src.shape[0] * n) ** (-0.5)
    me = lax.axis_index("space")

    below = edge_dst < reach
    inside = edge_dst < reach + mols
    target = jnp.where(below, edge_dst + mols, jnp.where(inside, edge_dst - reach, edge_dst))
    base = (mols + 2 * reach).bit_length()
    ids = jnp.where(edge_live > 0, (edge_src << base) + target, -1).reshape(n, cap)
    pack = 4 if half % 64 == 0 else 1
    tail_span = 128 // pack
    idx_own = lax.dynamic_slice_in_dim(ids, me, 1, axis=0)
    own_row = lax.broadcasted_iota(jnp.int32, (n, half), 0) == me
    idx = jnp.where(own_row, -1, ids[:, :half]).reshape(4, quarter, pack, half // pack)
    idx = idx.transpose(0, 2, 1, 3).reshape(4, 1, chunk)
    blocks = grad_blocks[0]
    rest = entries - width
    tails = jnp.pad(blocks[:, :half, width:], ((0, 0), (0, 0), (0, tail_span - rest)))
    tails = tails.reshape(n, pack, half // pack, tail_span).transpose(0, 2, 1, 3).reshape(n, half // pack, 128)

    span = mols + 2 * reach
    count = mols + span
    vm = pltpu.VMEM
    dma = pltpu.SemaphoreType.DMA
    scratch = [
        vm((cap, entries), BF16),
        vm((mols, width), BF16),
        vm((width, width), BF16),
        vm((width, width), BF16),
        vm((width, width), BF16),
        vm((width, tail_span), BF16),
        vm((2, reach, width), BF16),
        vm((span, width), BF16),
        vm((n, half, width), BF16),
        vm((n, half // pack, 128), BF16),
        vm((width, count), BF16),
        vm((width, count), BF16),
        vm((width, span), BF16),
        vm((4, count, chunk), BF16),
        vm((4, width, chunk), BF16),
        vm((4, width, chunk), F32),
        vm((count, cap), BF16),
        vm((width, cap), BF16),
        vm((width, cap), F32),
        vm((count, width), F32),
        vm((width, entries), F32),
        vm((2, reach, width), F32),
        dma((n,)), dma((n,)), dma((n,)), dma((n,)), dma((2,)), dma((2,)), dma((2,)), dma((2,)), dma((4,)),
    ]
    if fused:
        for columns in (entries, width, width):
            piece = (quarter, rows, columns)
            scratch += [
                vm((2, 2) + piece, F32),
                vm((2,) + piece, BF16),
                vm((2,) + piece, BF16),
                vm(piece, F32),
                vm(piece, BF16),
                vm(piece, BF16),
                vm(piece, BF16),
                vm(piece, BF16),
            ]
        scratch += [dma((3,)), dma((3,)), dma((3,)), dma((3,)), dma((3, quarter)), dma((3, quarter))]
    out_rows = rows if fused else width
    whole = pl.BlockSpec(memory_space=pltpu.VMEM)
    near = pl.BlockSpec(memory_space=pl.ANY)
    far = pl.BlockSpec(memory_space=pltpu.HBM)
    fgrad, src_g, dst_g, out_g = pl.pallas_call(
        functools.partial(kernel, (n, half, mols, reach, factor, fused, pack, base)),
        out_shape=(
            jax.ShapeDtypeStruct((mols, width), F32),
            jax.ShapeDtypeStruct((out_rows, width), F32),
            jax.ShapeDtypeStruct((out_rows, width), F32),
            jax.ShapeDtypeStruct((out_rows, entries), F32),
        ),
        in_specs=[far] * 3 + [whole] * 3 + [near] * 2,
        out_specs=(whole,) * 4,
        scratch_shapes=scratch,
        compiler_params=pltpu.CompilerParams(
            collective_id=0, has_side_effects=True, vmem_limit_bytes=48 * 1024 * 1024
        ),
    )(mol_feats, w_src, w_dst, w_out.T, idx, idx_own, blocks, tails)
    if not fused:
        src_g, dst_g, out_g = [
            lax.psum_scatter(part, "space", scatter_dimension=0, tiled=True) for part in (src_g, dst_g, out_g)
        ]
        return fgrad, src_g, dst_g, out_g
    results = (fgrad, src_g, dst_g, out_g)
    return pl.pallas_call(
        write_out,
        out_shape=tuple(jax.ShapeDtypeStruct(r.shape, r.dtype) for r in results),
        in_specs=[near] * 4,
        out_specs=(far,) * 4,
        scratch_shapes=[dma((4,))],
    )(*results)


def solution(mesh):
    placed = (
        P(("groups", "space"), None),
        P(),
        P(),
        P(),
        P("space", "groups", None, None),
        P(("groups", "space")),
        P(("groups", "space")),
        P(("groups", "space")),
    )
    return jax.shard_map(
        on_device,
        mesh=mesh,
        in_specs=placed,
        out_specs=(P(("groups", "space"), None),) * 4,
        check_vma=False,
    )
```

```python
import functools

import jax
import jax.numpy as jnp
from jax import lax
from jax.experimental import pallas as pl
from jax.experimental.pallas import tpu as pltpu
from jax.sharding import PartitionSpec as P

MESH = pl.DeviceIdType.MESH
F32 = jnp.float32
BF16 = jnp.bfloat16
NT = (((1,), (1,)), ((), ()))


def mm(a, b):
    return jnp.dot(a, b, preferred_element_type=F32)


def mm_nt(a, b):
    return lax.dot_general(a, b, NT, preferred_element_type=F32)


def split(x):
    high = x.astype(BF16)
    return high, (x - high.astype(F32)).astype(BF16)


def kernel(
    dims, feats_far, w_src_far, w_dst_far, w_out_t, idx, idx_own, blocks, fgrad, src_out, dst_out, out_out,
    own, mine, tails, feats, w_src, w_dst, w_main, w_tail, halo, ext, recv, recv_tail, pt_hi, pt_lo, ft, oh, hid, fac, oh_own, hid_own,
    fac_own, sums, out_sum, back, block_send, block_recv, tail_send, tail_recv, halo_send, halo_recv, back_send,
    back_recv, load_sem, *rs,
):
    n, half, mols, reach, factor, fused, pack, base = dims
    quarter = n // 4
    chunk = quarter * half
    width = w_main.shape[0]
    me = lax.axis_index("space")
    above = lax.rem(me + 1, n)
    below = lax.rem(me + n - 1, n)

    barrier = pltpu.get_barrier_semaphore()

    @pl.loop(1, n)
    def _(k):
        pl.semaphore_signal(barrier, inc=1, device_id={"space": lax.rem(me + k, n)}, device_id_type=MESH)

    pairs = ((feats_far, feats), (w_src_far, w_src), (w_dst_far, w_dst), (blocks.at[me], own), (blocks.at[:, pl.ds(0, half)], mine))
    loads = [pltpu.make_async_copy(far, near, load_sem.at[i]) for i, (far, near) in enumerate(pairs)]
    for load in loads:
        load.start()
    pl.semaphore_wait(barrier, n - 1)

    def remote(src, dst, send, arrive, device):
        return pltpu.make_async_remote_copy(
            src_ref=src, dst_ref=dst, send_sem=send, recv_sem=arrive,
            device_id={"space": device}, device_id_type=MESH,
        )

    def block_copy(source_slot, target):
        return remote(
            blocks.at[target, pl.ds(0, half), pl.ds(0, width)], recv.at[source_slot],
            block_send.at[target], block_recv.at[source_slot], target,
        )

    def tail_copy(source_slot, target):
        return remote(
            tails.at[target], recv_tail.at[source_slot], tail_send.at[target], tail_recv.at[source_slot], target
        )

    up = remote(feats_far.at[pl.ds(mols - reach, reach)], halo.at[0], halo_send.at[0], halo_recv.at[0], above)
    down = remote(feats_far.at[pl.ds(0, reach)], halo.at[1], halo_send.at[1], halo_recv.at[1], below)
    up.start()
    down.start()

    @pl.loop(1, n)
    def _(k):
        block_copy(me, lax.rem(me + k, n)).start()

    rest = w_out_t.shape[0] - width
    span = w_tail.shape[1]
    loads[4].wait()

    @pl.loop(1, n)
    def _(k):
        target = lax.rem(me + k, n)
        tail = mine[target, :, width:].astype(F32)
        tail = jnp.concatenate([tail, jnp.zeros((half, span - rest), F32)], axis=1)
        tail = tail.reshape(pack, half // pack, span)
        tails[target] = jnp.concatenate([tail[p] for p in range(pack)], axis=1).astype(BF16)
        tail_copy(me, target).start()

    recv[me] = jnp.zeros(recv.shape[1:], BF16)
    recv_tail[me] = jnp.zeros(recv_tail.shape[1:], BF16)
    w_main[...] = w_out_t[0:width].astype(F32).T.astype(BF16)
    last = w_out_t[width:].astype(F32)
    last = jnp.concatenate([last, jnp.zeros((w_tail.shape[1] - rest, width), F32)], axis=0)
    w_tail[...] = last.T.astype(BF16)
    for load in loads[0:4]:
        load.wait()
    ext[0:mols] = feats[...]
    pt = mm(feats[...], w_src[...]).T
    high, low = split(pt)
    pt_hi[:, 0:mols] = high
    pt_lo[:, 0:mols] = low
    up.wait()
    down.wait()
    ext[mols : mols + reach] = halo[0]
    ext[mols + reach : mols + 2 * reach] = halo[1]
    pt = mm(ext[...], w_dst[...]).T
    high, low = split(pt)
    pt_hi[:, mols:] = high
    pt_lo[:, mols:] = low
    ft[...] = ext[...].astype(F32).T.astype(BF16)

    def one_hot(ids, count):
        return (lax.broadcasted_iota(jnp.int32, (count, ids.shape[1]), 0) == ids).astype(F32).astype(BF16)

    def ahead(ids, oh_ref, hid_ref, fac_ref):
        oh_ref[0:mols] = one_hot(lax.shift_right_arithmetic(ids, base), mols)
        oh_ref[mols:] = one_hot(ids & ((1 << base) - 1), mols + 2 * reach)
        pre = mm(pt_hi[...], oh_ref[...]) + mm(pt_lo[...], oh_ref[...])
        sigma = jax.nn.sigmoid(pre)
        hid_ref[...] = (pre * sigma).astype(BF16)
        fac_ref[...] = sigma * (1.0 + pre * (1.0 - sigma))

    def terms(g, tail, oh_ref, hid_ref, fac_ref):
        dhidden = mm_nt(w_main[...], g) + mm_nt(w_tail[...], tail)
        dpre = (dhidden * fac_ref[...]).astype(BF16)
        return mm_nt(oh_ref[...], dpre), mm(hid_ref[...], g), mm(hid_ref[...], tail)[:, 0:rest]

    own_tail = jnp.concatenate(
        [own[:, width:].astype(F32), jnp.zeros((own.shape[0], w_tail.shape[1] - rest), F32)], axis=1
    ).astype(BF16)
    ahead(idx_own[...], oh_own, hid_own, fac_own)
    s, o, t = terms(own[:, 0:width], own_tail, oh_own, hid_own, fac_own)
    sums[...] = s
    out_sum[:, 0:width] = o
    out_sum[:, width:] = t

    @pl.loop(0, 4)
    def _(c):
        ahead(idx[c], oh.at[c], hid.at[c], fac.at[c])

    @pl.loop(0, 4)
    def _(k):
        c = lax.rem(me // quarter + k, 4)

        @pl.loop(0, quarter)
        def _(j):
            owner = c * quarter + j

            @pl.when(owner != me)
            def _():
                block_copy(owner, owner).wait_recv()
                tail_copy(owner, owner).wait_recv()

        g = recv[pl.ds(c * quarter, quarter)].reshape(quarter, pack, half // pack, width)
        g = jnp.concatenate([g[:, p].reshape(chunk // pack, width) for p in range(pack)], axis=0)
        tail = recv_tail[pl.ds(c * quarter, quarter)].reshape(chunk // pack, recv_tail.shape[2]).astype(F32)
        tail = jnp.concatenate([tail[:, p * span : (p + 1) * span] for p in range(pack)], axis=0).astype(BF16)
        s, o, t = terms(g, tail, oh.at[c], hid.at[c], fac.at[c])
        sums[...] += s
        out_sum[:, 0:width] += o
        out_sum[:, width:] += t

    give_down = remote(sums.at[pl.ds(2 * mols, reach)], back.at[1], back_send.at[0], back_recv.at[1], below)
    give_up = remote(sums.at[pl.ds(2 * mols + reach, reach)], back.at[0], back_send.at[1], back_recv.at[0], above)

    def source_grad():
        high, low = split(sums[0:mols])
        return (mm(ft[:, 0:mols], high) + mm(ft[:, 0:mols], low)) * factor

    def target_grad():
        high, low = split(sums[mols:])
        return (mm(ft[...], high) + mm(ft[...], low)) * factor

    def feature_part():
        high, low = split(sums[0:mols])
        fgrad[...] = mm_nt(high, w_src[...]) + mm_nt(low, w_src[...])

    def feature_rest():
        give_down.wait()
        give_up.wait()
        total = jnp.concatenate(
            [
                sums[mols : mols + reach] + back[0],
                sums[mols + reach : 2 * mols - reach],
                sums[2 * mols - reach : 2 * mols] + back[1],
            ],
            axis=0,
        )
        high, low = split(total)
        fgrad[...] += mm_nt(high, w_dst[...]) + mm_nt(low, w_dst[...])

    if fused:
        chains = [rs[8 * a : 8 * a + 8] for a in range(3)]
        send_a, recv_a, send_b, recv_b, send_c, recv_c = rs[24:]
        core = lax.rem(me, 2)
        row = lax.rem(me // 2, 2)
        column = me // 4
        rows = out_out.shape[0]

        def stage_a(a, value):
            full, s1, r1 = chains[a][:3]
            value = value.reshape(quarter, 2, 2, rows, value.shape[1])
            for y in range(2):
                for p in range(2):
                    full[p, y] = value[:, y, p]
            s1[...] = full[1 - core].astype(BF16)
            copy_a(a).start()

        def copy_a(a):
            return remote(chains[a][1], chains[a][2], send_a.at[a], recv_a.at[a], me + 1 - 2 * core)

        def copy_b(a):
            return remote(chains[a][4], chains[a][5], send_b.at[a], recv_b.at[a], me + 2 - 4 * row)

        def stage_b(a):
            full, s1, r1, keep, s2 = chains[a][:5]
            copy_a(a).wait()
            s2[...] = (full[core, 1 - row] + r1[1 - row].astype(F32)).astype(BF16)
            copy_b(a).start()
            keep[...] = full[core, row] + r1[row].astype(F32)

        def copy_c(a, slot, target):
            return remote(
                chains[a][6].at[target], chains[a][7].at[slot], send_c.at[a, target], recv_c.at[a, slot],
                target * 4 + lax.rem(me, 4),
            )

        def stage_c(a):
            keep, s2, r2, s3, r3 = chains[a][3:]
            copy_b(a).wait()
            total = keep[...] + r2[...].astype(F32)
            keep[...] = total
            s3[...] = total.astype(BF16)

            @pl.loop(1, quarter)
            def _(k):
                copy_c(a, column, lax.rem(column + k, quarter)).start()

        def stage_d(a, result):
            keep, s2, r2, s3, r3 = chains[a][3:]
            r3[column] = jnp.zeros(r3.shape[1:], BF16)

            @pl.loop(1, quarter)
            def _(k):
                other = lax.rem(column + k, quarter)
                copy_c(a, other, other).wait()

            total = keep[column]
            for z in range(quarter):
                total = total + r3[z].astype(F32)
            result[...] = total

        stage_a(0, out_sum[...] * factor)
        give_down.start()
        give_up.start()
        stage_a(1, source_grad())
        stage_b(0)
        stage_a(2, target_grad())
        stage_b(1)
        stage_c(0)
        stage_b(2)
        feature_part()
        stage_c(1)
        feature_rest()
        stage_c(2)
        stage_d(0, out_out)
        stage_d(1, src_out)
        stage_d(2, dst_out)
    else:
        give_down.start()
        give_up.start()
        out_out[...] = out_sum[...] * factor
        src_out[...] = source_grad()
        dst_out[...] = target_grad()
        feature_part()
        feature_rest()

    @pl.loop(1, n)
    def _(k):
        block_copy(me, lax.rem(me + k, n)).wait_send()
        tail_copy(me, lax.rem(me + k, n)).wait_send()


def on_device(mol_feats, w_src, w_dst, w_out, grad_blocks, edge_src, edge_dst, edge_live):
    mols, width = mol_feats.shape
    entries = w_out.shape[1]
    reach = mols // 4
    n = grad_blocks.shape[1]
    cap = grad_blocks.shape[2]
    half = cap // 2
    quarter = n // 4
    chunk = quarter * half
    rows = width // n
    fused = rows % 16 == 0
    factor = float(edge_src.shape[0] * n) ** (-0.5)
    me = lax.axis_index("space")

    below = edge_dst < reach
    inside = edge_dst < reach + mols
    target = jnp.where(below, edge_dst + mols, jnp.where(inside, edge_dst - reach, edge_dst))
    base = (mols + 2 * reach).bit_length()
    ids = jnp.where(edge_live > 0, (edge_src << base) + target, -1).reshape(n, cap)
    pack = 4 if half % 64 == 0 else 1
    tail_span = 128 // pack
    idx_own = lax.dynamic_slice_in_dim(ids, me, 1, axis=0)
    own_row = lax.broadcasted_iota(jnp.int32, (n, half), 0) == me
    idx = jnp.where(own_row, -1, ids[:, :half]).reshape(4, quarter, pack, half // pack)
    idx = idx.transpose(0, 2, 1, 3).reshape(4, 1, chunk)
    blocks = grad_blocks[0]

    span = mols + 2 * reach
    count = mols + span
    vm = pltpu.VMEM
    dma = pltpu.SemaphoreType.DMA
    scratch = [
        vm((cap, entries), BF16),
        vm((n, half, entries), BF16),
        vm((n, half // pack, 128), BF16),
        vm((mols, width), BF16),
        vm((width, width), BF16),
        vm((width, width), BF16),
        vm((width, width), BF16),
        vm((width, tail_span), BF16),
        vm((2, reach, width), BF16),
        vm((span, width), BF16),
        vm((n, half, width), BF16),
        vm((n, half // pack, 128), BF16),
        vm((width, count), BF16),
        vm((width, count), BF16),
        vm((width, span), BF16),
        vm((4, count, chunk), BF16),
        vm((4, width, chunk), BF16),
        vm((4, width, chunk), F32),
        vm((count, cap), BF16),
        vm((width, cap), BF16),
        vm((width, cap), F32),
        vm((count, width), F32),
        vm((width, entries), F32),
        vm((2, reach, width), F32),
        dma((n,)), dma((n,)), dma((n,)), dma((n,)), dma((2,)), dma((2,)), dma((2,)), dma((2,)), dma((5,)),
    ]
    if fused:
        for columns in (entries, width, width):
            piece = (quarter, rows, columns)
            scratch += [
                vm((2, 2) + piece, F32),
                vm((2,) + piece, BF16),
                vm((2,) + piece, BF16),
                vm(piece, F32),
                vm(piece, BF16),
                vm(piece, BF16),
                vm(piece, BF16),
                vm(piece, BF16),
            ]
        scratch += [dma((3,)), dma((3,)), dma((3,)), dma((3,)), dma((3, quarter)), dma((3, quarter))]
    out_rows = rows if fused else width
    whole = pl.BlockSpec(memory_space=pltpu.VMEM)
    near = pl.BlockSpec(memory_space=pl.ANY)
    far = pl.BlockSpec(memory_space=pltpu.HBM)
    fgrad, src_g, dst_g, out_g = pl.pallas_call(
        functools.partial(kernel, (n, half, mols, reach, factor, fused, pack, base)),
        out_shape=(
            jax.ShapeDtypeStruct((mols, width), F32),
            jax.ShapeDtypeStruct((out_rows, width), F32),
            jax.ShapeDtypeStruct((out_rows, width), F32),
            jax.ShapeDtypeStruct((out_rows, entries), F32),
        ),
        in_specs=[far] * 3 + [whole] * 3 + [near],
        out_specs=(whole,) * 4,
        scratch_shapes=scratch,
        compiler_params=pltpu.CompilerParams(
            collective_id=0, has_side_effects=True, vmem_limit_bytes=60 * 1024 * 1024
        ),
    )(mol_feats, w_src, w_dst, w_out.T, idx, idx_own, blocks)
    if not fused:
        src_g, dst_g, out_g = [
            lax.psum_scatter(part, "space", scatter_dimension=0, tiled=True) for part in (src_g, dst_g, out_g)
        ]
    return fgrad, src_g, dst_g, out_g


def solution(mesh):
    placed = (
        P(("groups", "space"), None),
        P(),
        P(),
        P(),
        P("space", "groups", None, None),
        P(("groups", "space")),
        P(("groups", "space")),
        P(("groups", "space")),
    )
    return jax.shard_map(
        on_device,
        mesh=mesh,
        in_specs=placed,
        out_specs=(P(("groups", "space"), None),) * 4,
        check_vma=False,
    )
```
